128 devices in a mesh: src: 16 (over y, z), rcv: 8 (over x, core).
Axes of the slice: x: 4, y: 4, z: 4, core: 2. Of those that a mesh axis runs over, the one named last changes fastest.
Arguments:
- traces: bfloat16 [2048, 1024], P('src', 'rcv'), may hold values from -300 to 300, as said below
- counts: int32 [16, 8], P('src', 'rcv'), may hold values from 1 to 4, as said below
- distances: int32 [4], replicated, may hold values from -8 to 7, as said below
Outputs:
- stacks: bfloat16 [16, 4, 64, 128, 2048], P('src', None, None, None, 'rcv')
The draws below stay inside these ranges and needn't reach their ends.
Inputs may be any that keep to these rules, and one draw needn't show every extreme that they name: `counts`: each entry is at least 1 and at most 4; both ends occur. 4 distinct block distances; -8, -1 and 7 always occur. `traces`: finite values.
All inputs are finite; a program needn't handle non-finite values.
Results may differ from the reference program's by a relative error of at most 0.0057.
Values may be sent and summed in bfloat16 or wider, within the bound.
No kernel may reach another device: no remote copies, remote signals or barrier semaphores. Data moves between devices by JAX's collectives and lax.ppermute only.
A program may use at most 384 MiB of HBM per device.

```python
import math
import jax
import jax.numpy as jnp
from jax import lax

CB = 128
LAGS = 2048
VS = 64
SEG = 128
WIN = 32
K = 4
NB = 16
N_RCV = 8


def draw_traces(key, part):
    key = jax.random.fold_in(key, 11)
    noise_key, scale_key = jax.random.split(key, 2)
    total_time = SEG * N_RCV
    channel_scale = jnp.exp(jax.random.uniform(scale_key, (NB * CB, 1), minval=0.0, maxval=math.log(10.0)))
    ramp = jnp.arange(total_time, dtype=jnp.float32) / total_time
    noise = jnp.clip(jax.random.normal(noise_key, (NB * CB, total_time)), -6.0, 6.0)
    envelope = jnp.exp(math.log(4.0) * ramp)[None, :]
    return (noise * envelope * channel_scale).astype(jnp.bfloat16)


def draw_counts(key, part):
    key = jax.random.fold_in(key, 23)
    drawn = jax.random.randint(key, (NB, N_RCV), 1, SEG // WIN + 1)
    drawn = drawn.at[0, 0].set(SEG // WIN)
    drawn = drawn.at[NB - 1, N_RCV - 1].set(1)
    return drawn.astype(jnp.int32)


def draw_distances(key, part):
    key = jax.random.fold_in(key, 37)
    inner_key, order_key = jax.random.split(key, 2)
    fixed_values = jnp.array([-(NB // 2), -1, NB // 2 - 1], jnp.int32)
    candidates = (jax.random.permutation(inner_key, NB) - NB // 2).astype(jnp.int32)
    taken = jnp.any(candidates[:, None] == fixed_values[None, :], axis=1)
    priority = jnp.where(taken, NB + jnp.arange(NB, dtype=jnp.int32), jnp.arange(NB, dtype=jnp.int32))
    order = jnp.argsort(priority, stable=True)
    extra = candidates[order[:K - 3]]
    chosen = jnp.concatenate([fixed_values, extra.astype(jnp.int32)])
    shuffle = jax.random.permutation(order_key, K)
    return chosen[shuffle].astype(jnp.int32)


def setup_inputs(seed: int = 0) -> dict:
    key_list = jax.random.split(jax.random.key(seed), 4)
    traces = draw_traces(jax.random.fold_in(key_list[3], 71), 0)
    counts = draw_counts(jax.random.fold_in(key_list[3], 71), 0)
    distances = draw_distances(jax.random.fold_in(key_list[3], 71), 0)
    return {"traces": traces, "counts": counts, "distances": distances}


def toeplitz(signals, lag_block):
    signal_count, duration = signals.shape
    padded = jnp.concatenate([signals, jnp.zeros((signal_count, lag_block + 1), signals.dtype)], axis=1)
    repeated = jnp.tile(padded, (1, lag_block))[:, :lag_block * (duration + lag_block)]
    return repeated.reshape(signal_count, lag_block, duration + lag_block)

def correlate(shifted, extended, lag_block):
    duration = shifted.shape[2]
    columns = []
    for lag_index in range(LAGS // lag_block):
        window_rows = extended[:, lag_index * lag_block:lag_index * lag_block + duration]
        columns.append(jnp.einsum('iux,jx->iju', shifted.astype(jnp.float32), window_rows.astype(jnp.float32)))
    return jnp.concatenate(columns, axis=2)

def reference(traces, counts, distances):
    values = traces.astype(jnp.float32)
    total_time = values.shape[1]
    energy = lax.optimization_barrier(jnp.sum(values * values, axis=1))
    inverse_rms = lax.rsqrt(energy / total_time + 1e-06)
    whitened = (values * inverse_rms[:, None]).astype(jnp.bfloat16)
    blocks = whitened.reshape(NB, CB, total_time)
    sample_index = jnp.arange(total_time, dtype=jnp.int32)
    kept_limit = jnp.repeat(counts * WIN, SEG, axis=1)
    kept_mask = (sample_index % SEG)[None, :] < kept_limit
    sources = jnp.where(kept_mask[:, None, :], blocks[:, :VS, :], jnp.zeros((), jnp.bfloat16))
    padded = jnp.pad(blocks, ((0, 0), (0, 0), (LAGS // 2, LAGS // 2)))
    lag_block = math.gcd(LAGS, 256)
    normalizer = jnp.sqrt((WIN * lax.optimization_barrier(jnp.sum(counts, axis=1))).astype(jnp.float32))

    def one_block(block_index):
        source_rows = lax.dynamic_index_in_dim(sources, block_index, 0, keepdims=False)
        shifted = toeplitz(source_rows, lag_block)
        results = []
        for slot_index in range(K):
            target = block_index + distances[slot_index]
            inside = jnp.logical_and(target >= 0, target < NB)
            partner = lax.dynamic_index_in_dim(padded, jnp.clip(target, 0, NB - 1).astype(jnp.int32), 0, keepdims=False)
            products = correlate(shifted, partner, lag_block)
            results.append(jnp.where(inside, products, jnp.zeros((), jnp.float32)))
        return jnp.stack(results)
    summed = lax.map(one_block, jnp.arange(NB, dtype=jnp.int32))
    return (summed / normalizer[:, None, None, None, None]).astype(jnp.bfloat16)
```

```python
import functools

import jax
import jax.numpy as jnp
from jax import lax
from jax.experimental import pallas as pl
from jax.experimental.pallas import tpu as pltpu
from jax.sharding import PartitionSpec as P

LAGS = 2048
VS = 64
WIN = 32
K = 4
CB = 128
SEG = 128
NB = 16
TIME = 1024
SHARE = 256
SPAN = TIME + SHARE
GROUP = 4
FIXED = (-8, -1, 7)
OTHERS = (-7, -6, -5, -4, -3, -2, 0, 1, 2, 3, 4, 5, 6)


def whiten(raw):
    values = raw.astype(jnp.float32)
    energy = jnp.sum(values * values, axis=1, keepdims=True)
    return (values * lax.rsqrt(energy / TIME + 1e-06)).astype(jnp.bfloat16)


def corr_kernel(dist_ref, own_ref, counts_ref, p0, p1, p2, p3, out_ref, w_ref, v_ref, t_ref, s_ref):
    step = pl.program_id(0)

    @pl.when(step == 0)
    def _():
        for s, p in enumerate((p0, p1, p2, p3)):
            w_ref[s * CB : (s + 1) * CB, :] = whiten(p[...])
        counts = counts_ref[0:1, :].astype(jnp.float32)
        s_ref[...] = lax.rsqrt(jnp.sum(counts, axis=1, keepdims=True) * (WIN / SEG))
        lane = lax.broadcasted_iota(jnp.int32, (1, TIME), 1)
        kept = (lane % SEG).astype(jnp.float32) < counts * WIN
        sources = jnp.where(kept, whiten(own_ref[0:VS, :]).astype(jnp.float32), 0.0).astype(jnp.bfloat16)
        row = lax.broadcasted_iota(jnp.int32, (SEG, SEG), 0)
        col = lax.broadcasted_iota(jnp.int32, (SEG, SEG), 1)
        flip = jnp.where(row + col == SEG - 1, 1.0, 0.0).astype(jnp.bfloat16)
        v_ref[...] = jnp.zeros_like(v_ref)
        for e in range(8):
            part = sources[:, (7 - e) * SEG : (8 - e) * SEG]
            v_ref[:, TIME + e * SEG : TIME + (e + 1) * SEG] = jnp.dot(
                part, flip, preferred_element_type=jnp.float32
            )

    own_part = lax.axis_index("rcv")
    base = pl.multiple_of(own_part * SHARE, SHARE)
    scale = s_ref[0:1, 0:1]
    slot_of = [jnp.int32(0)] * K
    rest = jnp.int32(0)
    for k in range(K):
        fixed = jnp.bool_(False)
        for s, d in enumerate(FIXED):
            hit = dist_ref[k] == d
            slot_of[s] = jnp.where(hit, k, slot_of[s])
            fixed = jnp.logical_or(fixed, hit)
        rest = jnp.where(fixed, rest, k)
    slot_of[3] = rest
    for ii in range(GROUP):
        row = v_ref[pl.ds(step * GROUP + ii, 1), pl.ds(base, SPAN)]
        z = pltpu.roll(
            jnp.broadcast_to(row, (16, SPAN)), SPAN - 15, 1, stride=1, stride_axis=0
        ).astype(jnp.bfloat16)
        tile = t_ref.at[ii % 2]
        for g in range(TIME // 16):
            at = TIME - 16 * (g + 1)
            tile[16 * g : 16 * g + 16, :] = z[:, at : at + SHARE]
        summed = jnp.dot(w_ref[...], tile[...], preferred_element_type=jnp.float32)
        stack = (summed * scale).astype(jnp.bfloat16)
        for s in range(K):
            out_ref[slot_of[s], ii] = stack[s * CB : (s + 1) * CB]


def correlate(distances, own, counts_rows, partners):
    vmem = pl.BlockSpec((CB, TIME), lambda i: (0, 0))
    return pl.pallas_call(
        corr_kernel,
        grid=(VS // GROUP,),
        in_specs=[
            pl.BlockSpec(memory_space=pltpu.SMEM),
            vmem,
            pl.BlockSpec((16, TIME), lambda i: (0, 0)),
            vmem,
            vmem,
            vmem,
            vmem,
        ],
        out_specs=pl.BlockSpec((K, GROUP, CB, SHARE), lambda i: (0, i, 0, 0)),
        out_shape=jax.ShapeDtypeStruct((K, VS, CB, SHARE), jnp.bfloat16),
        scratch_shapes=[
            pltpu.VMEM((K * CB, TIME), jnp.bfloat16),
            pltpu.VMEM((VS, 3 * TIME), jnp.float32),
            pltpu.VMEM((2, TIME, SHARE), jnp.bfloat16),
            pltpu.VMEM((1, 1), jnp.float32),
        ],
        compiler_params=pltpu.CompilerParams(vmem_limit_bytes=48 * 2**20),
        name="corr",
    )(distances, own, counts_rows, *partners)


def shift(d):
    return [(p + d, p) for p in range(NB) if 0 <= p + d < NB]


def gather_rcv(x):
    core = lax.axis_index("rcv") % 2
    chip = lax.axis_index("rcv") // 2
    other = lax.ppermute(x, "rcv", [(s, s ^ 1) for s in range(8)])
    first = jnp.where(core == 0, x, other)
    second = jnp.where(core == 0, other, x)
    pair = jnp.concatenate([first, second], axis=1)
    turned = [pair] + [
        lax.ppermute(pair, "rcv", [((s + 2 * d) % 8, s) for s in range(8)]) for d in (1, 2, 3)
    ]
    whole = jnp.zeros((x.shape[0], TIME), x.dtype)
    for d in range(4):
        whole = lax.dynamic_update_slice(whole, turned[d], (0, (chip + d) % 4 * 256))
    return whole


def on_device(traces, counts, distances):
    rows = jnp.concatenate(
        [traces, jnp.broadcast_to(counts.astype(jnp.bfloat16), (16, SEG))], axis=0
    )
    whole = gather_rcv(rows)
    own = whole[:CB]
    partners = [lax.ppermute(own, "src", shift(d)) for d in FIXED]
    fourth = jnp.sum(distances) - sum(FIXED)
    branch = jnp.where(fourth < 0, fourth + 7, fourth + 6)
    moves = [
        (lambda y: y) if d == 0 else functools.partial(lax.ppermute, axis_name="src", perm=shift(d))
        for d in OTHERS
    ]
    partners.append(lax.switch(branch, moves, own))
    return correlate(distances, own, whole[CB:], partners)[None]


def solution(mesh):
    in_specs = (P("src", "rcv"), P("src", "rcv"), P())
    out_specs = P("src", None, None, None, "rcv")
    return jax.shard_map(
        on_device, mesh=mesh, in_specs=in_specs, out_specs=out_specs, check_vma=False
    )
```

```python
import functools

import jax
import jax.numpy as jnp
from jax import lax
from jax.experimental import pallas as pl
from jax.experimental.pallas import tpu as pltpu
from jax.sharding import PartitionSpec as P

LAGS = 2048
VS = 64
WIN = 32
K = 4
CB = 128
SEG = 128
NB = 16
N_RCV = 8
TIME = 1024
SHARE = 256
SPAN = TIME + SHARE
GROUP = 8
COPIES = 16
FIXED = (-8, -1, 7)
OTHERS = (-7, -6, -5, -4, -3, -2, 0, 1, 2, 3, 4, 5, 6)
VMEM_BYTES = 56 * 2**20


def whiten(raw, factor=None):
    values = raw.astype(jnp.float32)
    energy = jnp.sum(values * values, axis=1, keepdims=True)
    scale = lax.rsqrt(energy / TIME + 1e-06)
    if factor is not None:
        scale = scale * factor
    return (values * scale).astype(jnp.bfloat16)


def prepare_kernel(own_ref, copies_ref, scale_ref, v_ref):
    step = pl.program_id(0)

    @pl.when(step == 0)
    def _():
        counts = own_ref[CB : CB + 16, :].astype(jnp.float32)[0:1]
        norm = lax.rsqrt(jnp.sum(counts, axis=1, keepdims=True) * (WIN / SEG))
        scale_ref[...] = jnp.broadcast_to(norm, scale_ref.shape)
        lane = lax.broadcasted_iota(jnp.int32, (1, TIME), 1)
        kept = (lane % SEG).astype(jnp.float32) < counts * WIN
        sources = jnp.where(kept, whiten(own_ref[0:VS, :]).astype(jnp.float32), 0.0)
        sources = sources.astype(jnp.bfloat16)
        row = lax.broadcasted_iota(jnp.int32, (SEG, SEG), 0)
        col = lax.broadcasted_iota(jnp.int32, (SEG, SEG), 1)
        flip = jnp.where(row + col == SEG - 1, 1.0, 0.0).astype(jnp.bfloat16)
        v_ref[:, 0:TIME] = jnp.zeros((VS, TIME), jnp.float32)
        v_ref[:, 2 * TIME :] = jnp.zeros((VS, TIME), jnp.float32)
        for e in range(N_RCV):
            part = sources[:, (N_RCV - 1 - e) * SEG : (N_RCV - e) * SEG]
            v_ref[:, TIME + e * SEG : TIME + (e + 1) * SEG] = jnp.dot(
                part, flip, preferred_element_type=jnp.float32
            )

    base = pl.multiple_of(lax.axis_index("rcv") * SHARE, SHARE)
    first = pl.multiple_of(step * COPIES, COPIES)
    rows = v_ref[pl.ds(first, COPIES), pl.ds(base, SPAN)]
    spread = jnp.broadcast_to(rows[:, None, :], (COPIES, 16, SPAN))
    copies_ref[...] = pltpu.roll(spread, SPAN - 15, 2, stride=1, stride_axis=1).astype(jnp.bfloat16)


def prepare(whole):
    return pl.pallas_call(
        prepare_kernel,
        grid=(VS // COPIES,),
        in_specs=[pl.BlockSpec((CB + 16, TIME), lambda i: (0, 0))],
        out_specs=[
            pl.BlockSpec((COPIES, 16, SPAN), lambda i: (i, 0, 0)),
            pl.BlockSpec((8, 128), lambda i: (0, 0)),
        ],
        out_shape=[
            jax.ShapeDtypeStruct((VS, 16, SPAN), jnp.bfloat16),
            jax.ShapeDtypeStruct((8, 128), jnp.float32),
        ],
        scratch_shapes=[pltpu.VMEM((VS, 3 * TIME), jnp.float32)],
        compiler_params=pltpu.CompilerParams(vmem_limit_bytes=VMEM_BYTES),
        name="prepare",
    )(whole)


def corr_kernel(dist_ref, copies_ref, scale_ref, a1, b1, a2, b2, out_ref, w_ref, q_ref):
    core = lax.axis_index("rcv") % 2
    block = lax.axis_index("src")
    slot_of = [jnp.int32(0)] * K
    rest = jnp.int32(0)
    fourth = jnp.int32(0)
    for k in range(K):
        d = dist_ref[k]
        fixed = jnp.bool_(False)
        for s, known in enumerate(FIXED):
            hit = d == known
            slot_of[s] = jnp.where(hit, k, slot_of[s])
            fixed = jnp.logical_or(fixed, hit)
        rest = jnp.where(fixed, rest, k)
        fourth = jnp.where(fixed, fourth, d)
    slot_of[3] = rest
    order = ((0, 1), (1, 0), (2, 3), (3, 2))
    values = (*(jnp.int32(d) for d in FIXED), fourth)
    slots = [jnp.where(core == 0, slot_of[x], slot_of[y]) for x, y in order]

    @pl.when(pl.program_id(0) == 0)
    def _():
        for s, ((x, y), p) in enumerate(zip(order, (a1, b1, a2, b2))):
            partner = block + jnp.where(core == 0, values[x], values[y])
            inside = jnp.logical_and(partner >= 0, partner < NB)
            factor = jnp.where(inside, 1.0, 0.0).astype(jnp.float32)
            w_ref[s * CB : (s + 1) * CB, :] = whiten(p[...], factor)

    scale = scale_ref[0:1, 0:1]
    for ii in range(GROUP):
        copies = copies_ref[ii]
        blocks = q_ref.at[ii % 2]
        for g in range(8):
            at = 112 - 16 * g
            moved = copies[:, at : at + TIME + SEG]
            for c in range(9):
                blocks[SEG * c + 16 * g : SEG * c + 16 * g + 16, :] = moved[
                    :, SEG * (8 - c) : SEG * (9 - c)
                ]
        tile = jnp.concatenate([blocks[SEG : SEG + TIME], blocks[0:TIME]], axis=1)
        summed = jnp.dot(w_ref[...], tile, preferred_element_type=jnp.float32)
        stack = (summed * scale).astype(jnp.bfloat16)
        for s in range(K):
            out_ref[slots[s], ii] = stack[s * CB : (s + 1) * CB]


def correlate(distances, copies, scale, partners):
    vmem = pl.BlockSpec((CB, TIME), lambda i: (0, 0))
    return pl.pallas_call(
        corr_kernel,
        grid=(VS // GROUP,),
        in_specs=[
            pl.BlockSpec(memory_space=pltpu.SMEM),
            pl.BlockSpec((GROUP, 16, SPAN), lambda i: (i, 0, 0)),
            pl.BlockSpec((8, 128), lambda i: (0, 0)),
            vmem,
            vmem,
            vmem,
            vmem,
        ],
        out_specs=pl.BlockSpec((K, GROUP, CB, SHARE), lambda i: (0, i, 0, 0)),
        out_shape=jax.ShapeDtypeStruct((K, VS, CB, SHARE), jnp.bfloat16),
        scratch_shapes=[
            pltpu.VMEM((K * CB, TIME), jnp.bfloat16),
            pltpu.VMEM((2, TIME + SEG, SEG), jnp.bfloat16),
        ],
        compiler_params=pltpu.CompilerParams(vmem_limit_bytes=VMEM_BYTES),
        name="corr",
    )(distances, copies, scale, *partners)


SWAP = [(s, s ^ 1) for s in range(N_RCV)]


def gather_rcv(x, branch):
    core = lax.axis_index("rcv") % 2
    chip = lax.axis_index("rcv") // 2
    other = lax.ppermute(x, "rcv", SWAP)
    x, other, branch = lax.optimization_barrier((x, other, branch))
    first = jnp.where(core == 0, x, other)
    second = jnp.where(core == 0, other, x)
    pair = jnp.concatenate([first, second], axis=1)
    turned = [pair] + [
        lax.ppermute(pair, "rcv", [((s + 2 * d) % 8, s) for s in range(8)]) for d in (1, 2, 3)
    ]
    whole = jnp.zeros((x.shape[0], TIME), x.dtype)
    for d in range(4):
        whole = lax.dynamic_update_slice(whole, turned[d], (0, (chip + d) % 4 * 256))
    return whole, branch


def fetch(y, even, odd):
    pairs = [
        ((p + (odd if m % 2 else even)) % NB * N_RCV + m, p * N_RCV + m)
        for p in range(NB)
        for m in range(N_RCV)
    ]
    return lax.ppermute(y, ("src", "rcv"), pairs)


def on_device(traces, counts, distances):
    fourth = jnp.sum(distances) - sum(FIXED)
    branch = jnp.where(fourth < 0, fourth + 7, fourth + 6)
    rows = jnp.concatenate(
        [traces, jnp.broadcast_to(counts.astype(jnp.bfloat16), (16, SEG))], axis=0
    )
    whole, branch = gather_rcv(rows, branch)
    own = whole[:CB]
    a1 = fetch(own, -8, -1)
    a2 = lax.switch(branch, [functools.partial(fetch, even=7, odd=d) for d in OTHERS], own)
    b1 = lax.ppermute(a1, "rcv", SWAP)
    b2 = lax.ppermute(a2, "rcv", SWAP)
    whole, a2 = lax.optimization_barrier((whole, a2))
    copies, scale = prepare(whole)
    return correlate(distances, copies, scale, (a1, b1, a2, b2))[None]


def solution(mesh):
    in_specs = (P("src", "rcv"), P("src", "rcv"), P())
    out_specs = P("src", None, None, None, "rcv")
    return jax.shard_map(
        on_device, mesh=mesh, in_specs=in_specs, out_specs=out_specs, check_vma=False
    )
```

```python
import functools

import jax
import jax.numpy as jnp
from jax import lax
from jax.experimental import pallas as pl
from jax.experimental.pallas import tpu as pltpu
from jax.sharding import PartitionSpec as P

LAGS = 2048
VS = 64
WIN = 32
K = 4
CB = 128
SEG = 128
NB = 16
N_RCV = 8
TIME = 1024
SHARE = 256
HALF = 512
SPAN = TIME + SHARE
GROUP = 8
COPIES = 16
FIXED = (-8, -1, 7)
OTHERS = (-7, -6, -5, -4, -3, -2, 0, 1, 2, 3, 4, 5, 6)
VMEM_BYTES = 32 * 2**20


def whiten(raw):
    values = raw.astype(jnp.float32)
    energy = jnp.sum(values * values, axis=1, keepdims=True)
    return (values * lax.rsqrt(energy / TIME + 1e-06)).astype(jnp.bfloat16)


def half_places():
    half = lax.axis_index("rcv") // 4
    return pl.multiple_of(half * HALF, HALF), pl.multiple_of((1 - half) * HALF, HALF)


def prepare_kernel(near_ref, far_ref, copies_ref, scale_ref, v_ref, own_ref):
    step = pl.program_id(0)

    @pl.when(step == 0)
    def _():
        near, far = half_places()
        own_ref[:, pl.ds(near, HALF)] = near_ref[...]
        own_ref[:, pl.ds(far, HALF)] = far_ref[...]
        counts = own_ref[CB : CB + 16, :].astype(jnp.float32)[0:1]
        norm = lax.rsqrt(jnp.sum(counts, axis=1, keepdims=True) * (WIN / SEG))
        scale_ref[...] = jnp.broadcast_to(norm, scale_ref.shape)
        lane = lax.broadcasted_iota(jnp.int32, (1, TIME), 1)
        kept = (lane % SEG).astype(jnp.float32) < counts * WIN
        sources = jnp.where(kept, whiten(own_ref[0:VS, :]).astype(jnp.float32), 0.0)
        sources = sources.astype(jnp.bfloat16)
        row = lax.broadcasted_iota(jnp.int32, (SEG, SEG), 0)
        col = lax.broadcasted_iota(jnp.int32, (SEG, SEG), 1)
        flip = jnp.where(row + col == SEG - 1, 1.0, 0.0).astype(jnp.bfloat16)
        v_ref[:, 0:TIME] = jnp.zeros((VS, TIME), jnp.float32)
        v_ref[:, 2 * TIME :] = jnp.zeros((VS, TIME), jnp.float32)
        for e in range(N_RCV):
            part = sources[:, (N_RCV - 1 - e) * SEG : (N_RCV - e) * SEG]
            v_ref[:, TIME + e * SEG : TIME + (e + 1) * SEG] = jnp.dot(
                part, flip, preferred_element_type=jnp.float32
            )

    base = pl.multiple_of(lax.axis_index("rcv") * SHARE, SHARE)
    first = pl.multiple_of(step * COPIES, COPIES)
    rows = v_ref[pl.ds(first, COPIES), pl.ds(base, SPAN)]
    spread = jnp.broadcast_to(rows[:, None, :], (COPIES, 16, SPAN))
    copies_ref[...] = pltpu.roll(spread, SPAN - 15, 2, stride=1, stride_axis=1).astype(jnp.bfloat16)


def prepare(near, far):
    return pl.pallas_call(
        prepare_kernel,
        grid=(VS // COPIES,),
        in_specs=[pl.BlockSpec((CB + 16, HALF), lambda i: (0, 0))] * 2,
        out_specs=[
            pl.BlockSpec((COPIES, 16, SPAN), lambda i: (i, 0, 0)),
            pl.BlockSpec((8, 128), lambda i: (0, 0)),
        ],
        out_shape=[
            jax.ShapeDtypeStruct((VS, 16, SPAN), jnp.bfloat16),
            jax.ShapeDtypeStruct((8, 128), jnp.float32),
        ],
        scratch_shapes=[
            pltpu.VMEM((VS, 3 * TIME), jnp.float32),
            pltpu.VMEM((CB + 16, TIME), jnp.bfloat16),
        ],
        compiler_params=pltpu.CompilerParams(vmem_limit_bytes=VMEM_BYTES),
        name="prepare",
    )(near, far)


def corr_kernel(dist_ref, copies_ref, scale_ref, *refs):
    *halves, out_ref, w_ref, q_ref = refs
    core = lax.axis_index("rcv") % 2
    block = lax.axis_index("src")
    slot_of = [jnp.int32(0)] * K
    rest = jnp.int32(0)
    fourth = jnp.int32(0)
    for k in range(K):
        d = dist_ref[k]
        fixed = jnp.bool_(False)
        for s, known in enumerate(FIXED):
            hit = d == known
            slot_of[s] = jnp.where(hit, k, slot_of[s])
            fixed = jnp.logical_or(fixed, hit)
        rest = jnp.where(fixed, rest, k)
        fourth = jnp.where(fixed, fourth, d)
    slot_of[3] = rest
    order = ((0, 1), (2, 3), (1, 0), (3, 2))
    values = (*(jnp.int32(d) for d in FIXED), fourth)
    inside = []
    for x, y in order:
        partner = block + jnp.where(core == 0, values[x], values[y])
        inside.append(jnp.logical_and(partner >= 0, partner < NB).astype(jnp.int32))
    total = sum(inside)
    ranks = []
    used, unused = jnp.int32(0), total
    for flag in inside:
        ranks.append(jnp.where(flag == 1, used, unused))
        used, unused = used + flag, unused + 1 - flag
    slots = [jnp.int32(0)] * K
    for s, (x, y) in enumerate(order):
        slot = jnp.where(core == 0, slot_of[x], slot_of[y])
        for r in range(K):
            slots[r] = jnp.where(ranks[s] == r, slot, slots[r])

    @pl.when(pl.program_id(0) == 0)
    def _():
        near, far = half_places()
        for s in range(K):
            first = halves[2 * s][...].astype(jnp.float32)
            second = halves[2 * s + 1][...].astype(jnp.float32)
            energy = jnp.sum(first * first + second * second, axis=1, keepdims=True)
            scale = lax.rsqrt(energy / TIME + 1e-06) * inside[s].astype(jnp.float32)
            rows = pl.ds(pl.multiple_of(ranks[s] * CB, CB), CB)
            w_ref[rows, pl.ds(near, HALF)] = (first * scale).astype(jnp.bfloat16)
            w_ref[rows, pl.ds(far, HALF)] = (second * scale).astype(jnp.bfloat16)

    scale = scale_ref[0:1, 0:1]

    def multiply(live):
        for ii in range(GROUP):
            copies = copies_ref[ii]
            blocks = q_ref.at[ii % 2]
            for g in range(8):
                at = 112 - 16 * g
                moved = copies[:, at : at + TIME + SEG]
                for c in range(9):
                    blocks[SEG * c + 16 * g : SEG * c + 16 * g + 16, :] = moved[
                        :, SEG * (8 - c) : SEG * (9 - c)
                    ]
            tile = jnp.concatenate([blocks[SEG : SEG + TIME], blocks[0:TIME]], axis=1)
            summed = jnp.dot(w_ref[: live * CB], tile, preferred_element_type=jnp.float32)
            stack = (summed * scale).astype(jnp.bfloat16)
            for r in range(K):
                if r < live:
                    out_ref[slots[r], ii] = stack[r * CB : (r + 1) * CB]
                else:
                    out_ref[slots[r], ii] = jnp.zeros((CB, SHARE), jnp.bfloat16)

    pl.when(total <= 2)(lambda: multiply(2))
    pl.when(total == 3)(lambda: multiply(3))
    pl.when(total == 4)(lambda: multiply(4))


def correlate(distances, copies, scale, halves):
    vmem = pl.BlockSpec((CB, HALF), lambda i: (0, 0))
    return pl.pallas_call(
        corr_kernel,
        grid=(VS // GROUP,),
        in_specs=[
            pl.BlockSpec(memory_space=pltpu.SMEM),
            pl.BlockSpec((GROUP, 16, SPAN), lambda i: (i, 0, 0)),
            pl.BlockSpec((8, 128), lambda i: (0, 0)),
            *([vmem] * len(halves)),
        ],
        out_specs=pl.BlockSpec((K, GROUP, CB, SHARE), lambda i: (0, i, 0, 0)),
        out_shape=jax.ShapeDtypeStruct((K, VS, CB, SHARE), jnp.bfloat16),
        scratch_shapes=[
            pltpu.VMEM((K * CB, TIME), jnp.bfloat16),
            pltpu.VMEM((2, TIME + SEG, SEG), jnp.bfloat16),
        ],
        compiler_params=pltpu.CompilerParams(vmem_limit_bytes=VMEM_BYTES),
        name="corr",
    )(distances, copies, scale, *halves)


def flip_rcv(x, bits):
    return lax.ppermute(x, "rcv", [(s, s ^ bits) for s in range(N_RCV)])


def own_half(x):
    place = lax.axis_index("rcv") % 4
    others = [flip_rcv(x, bits) for bits in (1, 2, 3)]
    half = jnp.zeros((x.shape[0], HALF), x.dtype)
    for bits, part in enumerate((x, *others)):
        half = lax.dynamic_update_slice(half, part, (0, (place ^ bits) * SEG))
    return half


def fetch(y, even, odd):
    pairs = [
        ((p + (odd if m % 2 else even)) % NB * N_RCV + m, p * N_RCV + m)
        for p in range(NB)
        for m in range(N_RCV)
    ]
    return lax.ppermute(y, ("src", "rcv"), pairs)


def second_fetch(own, a1, fourth):
    a2 = fetch(own, 7, fourth)
    return a2, flip_rcv(a1, 6), flip_rcv(a1, 1)


def on_device(traces, counts, distances):
    rows = jnp.concatenate(
        [traces, jnp.broadcast_to(counts.astype(jnp.bfloat16), (16, SEG))], axis=0
    )
    half = own_half(rows)
    own = half[:CB]
    a1 = fetch(own, -8, -1)
    far_half = flip_rcv(half, 6)
    fourth = jnp.sum(distances) - sum(FIXED)
    branch = jnp.where(fourth < 0, fourth + 7, fourth + 6)
    branch, a1, far_half = lax.optimization_barrier((branch, a1, far_half))
    moves = [functools.partial(second_fetch, fourth=d) for d in OTHERS]
    a2, c1, s1 = lax.switch(branch, moves, own, a1)
    c2 = flip_rcv(a2, 6)
    s2 = flip_rcv(a2, 1)
    r1 = flip_rcv(c1, 1)
    half, far_half, a2 = lax.optimization_barrier((half, far_half, a2))
    copies, scale = prepare(half, far_half)
    c2, copies = lax.optimization_barrier((c2, copies))
    r2 = flip_rcv(c2, 1)
    halves = (a1, c1, a2, c2, s1, r1, s2, r2)
    return correlate(distances, copies, scale, halves)[None]


def solution(mesh):
    in_specs = (P("src", "rcv"), P("src", "rcv"), P())
    out_specs = P("src", None, None, None, "rcv")
    return jax.shard_map(
        on_device, mesh=mesh, in_specs=in_specs, out_specs=out_specs, check_vma=False
    )
```

```python
import functools

import jax
import jax.numpy as jnp
from jax import lax
from jax.experimental import pallas as pl
from jax.experimental.pallas import tpu as pltpu
from jax.sharding import PartitionSpec as P

LAGS = 2048
VS = 64
WIN = 32
K = 4
CB = 128
SEG = 128
NB = 16
N_RCV = 8
TIME = 1024
SHARE = 256
HALF = 512
SPAN = TIME + SHARE
GROUP = 8
COPIES = 16
FIXED = (-8, -1, 7)
OTHERS = (-7, -6, -5, -4, -3, -2, 0, 1, 2, 3, 4, 5, 6)
VMEM_BYTES = 32 * 2**20


def whiten(raw):
    values = raw.astype(jnp.float32)
    energy = jnp.sum(values * values, axis=1, keepdims=True)
    return (values * lax.rsqrt(energy / TIME + 1e-06)).astype(jnp.bfloat16)


def at_end():
    part = lax.axis_index("rcv")
    return jnp.logical_or(part < 2, part >= N_RCV - 2)


def half_places(packed):
    half = lax.axis_index("rcv") // 4
    near = half * HALF
    if packed:
        near = jnp.where(at_end(), 0, near)
    return pl.multiple_of(near, HALF), pl.multiple_of(HALF - near, HALF)


def prepare_kernel(dist_ref, near_ref, far_ref, copies_ref, scale_ref, v_ref, own_ref):
    step = pl.program_id(0)

    @pl.when(step == 0)
    def _():
        near, far = half_places(False)
        own_ref[:, pl.ds(near, HALF)] = near_ref[...]
        own_ref[:, pl.ds(far, HALF)] = far_ref[...]
        counts = own_ref[CB : CB + 16, :].astype(jnp.float32)[0:1]
        norm = lax.rsqrt(jnp.sum(counts, axis=1, keepdims=True) * (WIN / SEG))
        line = lax.broadcasted_iota(jnp.int32, scale_ref.shape, 0)
        table = jnp.broadcast_to(norm, scale_ref.shape)
        for k in range(K):
            table = jnp.where(line == k + 1, dist_ref[k].astype(jnp.float32), table)
        scale_ref[...] = table
        lane = lax.broadcasted_iota(jnp.int32, (1, TIME), 1)
        kept = (lane % SEG).astype(jnp.float32) < counts * WIN
        sources = jnp.where(kept, whiten(own_ref[0:VS, :]).astype(jnp.float32), 0.0)
        sources = sources.astype(jnp.bfloat16)
        row = lax.broadcasted_iota(jnp.int32, (SEG, SEG), 0)
        col = lax.broadcasted_iota(jnp.int32, (SEG, SEG), 1)
        flip = jnp.where(row + col == SEG - 1, 1.0, 0.0).astype(jnp.bfloat16)
        v_ref[:, 0:TIME] = jnp.zeros((VS, TIME), jnp.float32)
        v_ref[:, 2 * TIME :] = jnp.zeros((VS, TIME), jnp.float32)
        for e in range(N_RCV):
            part = sources[:, (N_RCV - 1 - e) * SEG : (N_RCV - e) * SEG]
            v_ref[:, TIME + e * SEG : TIME + (e + 1) * SEG] = jnp.dot(
                part, flip, preferred_element_type=jnp.float32
            )

    part = lax.axis_index("rcv")
    late = jnp.where(part >= N_RCV - 2, HALF, 0)
    base = pl.multiple_of(part * SHARE - late, SHARE)
    first = pl.multiple_of(step * COPIES, COPIES)
    rows = v_ref[pl.ds(first, COPIES), pl.ds(base, SPAN)]
    spread = jnp.broadcast_to(rows[:, None, :], (COPIES, 16, SPAN))
    copies_ref[...] = pltpu.roll(spread, SPAN - 15, 2, stride=1, stride_axis=1).astype(jnp.bfloat16)


def prepare(distances, near, far):
    return pl.pallas_call(
        prepare_kernel,
        grid=(VS // COPIES,),
        in_specs=[
            pl.BlockSpec(memory_space=pltpu.SMEM),
            *[pl.BlockSpec((CB + 16, HALF), lambda i: (0, 0))] * 2,
        ],
        out_specs=[
            pl.BlockSpec((COPIES, 16, SPAN), lambda i: (i, 0, 0)),
            pl.BlockSpec((8, 128), lambda i: (0, 0)),
        ],
        out_shape=[
            jax.ShapeDtypeStruct((VS, 16, SPAN), jnp.bfloat16),
            jax.ShapeDtypeStruct((8, 128), jnp.float32),
        ],
        scratch_shapes=[
            pltpu.VMEM((VS, 3 * TIME), jnp.float32),
            pltpu.VMEM((CB + 16, TIME), jnp.bfloat16),
        ],
        compiler_params=pltpu.CompilerParams(vmem_limit_bytes=VMEM_BYTES),
        name="prepare",
    )(distances, near, far)


def corr_kernel(copies_ref, scale_ref, *refs):
    *halves, out_ref, w_ref, q_ref, plan_ref = refs

    @pl.when(pl.program_id(0) == 0)
    def _():
        core = lax.axis_index("rcv") % 2
        block = lax.axis_index("src")
        slot_of = [jnp.int32(0)] * K
        rest = jnp.int32(0)
        fourth = jnp.int32(0)
        for k in range(K):
            d = jnp.max(scale_ref[k + 1 : k + 2, :]).astype(jnp.int32)
            fixed = jnp.bool_(False)
            for s, known in enumerate(FIXED):
                hit = d == known
                slot_of[s] = jnp.where(hit, k, slot_of[s])
                fixed = jnp.logical_or(fixed, hit)
            rest = jnp.where(fixed, rest, k)
            fourth = jnp.where(fixed, fourth, d)
        slot_of[3] = rest
        order = ((0, 1), (2, 3), (1, 0), (3, 2))
        values = (*(jnp.int32(d) for d in FIXED), fourth)
        inside = []
        for x, y in order:
            partner = block + jnp.where(core == 0, values[x], values[y])
            inside.append(jnp.logical_and(partner >= 0, partner < NB).astype(jnp.int32))
        total = sum(inside)
        plan_ref[K] = total
        near, far = half_places(True)
        used, unused = jnp.int32(0), total
        for s, (x, y) in enumerate(order):
            rank = jnp.where(inside[s] == 1, used, unused)
            used, unused = used + inside[s], unused + 1 - inside[s]
            plan_ref[rank] = jnp.where(core == 0, slot_of[x], slot_of[y])
            first = halves[2 * s][...].astype(jnp.float32)
            second = halves[2 * s + 1][...].astype(jnp.float32)
            energy = jnp.sum(first * first + second * second, axis=1, keepdims=True)
            scale = lax.rsqrt(energy / TIME + 1e-06) * inside[s].astype(jnp.float32)
            rows = pl.ds(pl.multiple_of(rank * CB, CB), CB)
            w_ref[rows, pl.ds(near, HALF)] = (first * scale).astype(jnp.bfloat16)
            w_ref[rows, pl.ds(far, HALF)] = (second * scale).astype(jnp.bfloat16)

    scale = scale_ref[0:1, 0:1]
    slots = [plan_ref[r] for r in range(K)]
    total = plan_ref[K]
    end = at_end()

    def multiply(live, depth):
        count = depth // SEG + 1
        for ii in range(GROUP):
            copies = copies_ref[ii]
            blocks = q_ref.at[ii % 2]
            for g in range(8):
                for c in range(count):
                    at = 112 - 16 * g + SEG * (8 - c)
                    blocks[SEG * c + 16 * g : SEG * c + 16 * g + 16, :] = copies[:, at : at + SEG]
            tile = jnp.concatenate([blocks[SEG : SEG + depth], blocks[0:depth]], axis=1)
            summed = jnp.dot(
                w_ref[: live * CB, :depth], tile, preferred_element_type=jnp.float32
            )
            stack = (summed * scale).astype(jnp.bfloat16)
            for r in range(K):
                if r < live:
                    out_ref[slots[r], ii] = stack[r * CB : (r + 1) * CB]
                else:
                    out_ref[slots[r], ii] = jnp.zeros((CB, SHARE), jnp.bfloat16)

    for live in (2, 3, 4):
        fits = total <= 2 if live == 2 else total == live
        pl.when(jnp.logical_and(fits, end))(functools.partial(multiply, live, HALF))
        pl.when(jnp.logical_and(fits, jnp.logical_not(end)))(
            functools.partial(multiply, live, TIME)
        )


def correlate(copies, scale, halves):
    vmem = pl.BlockSpec((CB, HALF), lambda i: (0, 0))
    return pl.pallas_call(
        corr_kernel,
        grid=(VS // GROUP,),
        in_specs=[
            pl.BlockSpec((GROUP, 16, SPAN), lambda i: (i, 0, 0)),
            pl.BlockSpec((8, 128), lambda i: (0, 0)),
            *([vmem] * len(halves)),
        ],
        out_specs=pl.BlockSpec((K, GROUP, CB, SHARE), lambda i: (0, i, 0, 0)),
        out_shape=jax.ShapeDtypeStruct((K, VS, CB, SHARE), jnp.bfloat16),
        scratch_shapes=[
            pltpu.VMEM((K * CB, TIME), jnp.bfloat16),
            pltpu.VMEM((2, TIME + SEG, SEG), jnp.bfloat16),
            pltpu.SMEM((8,), jnp.int32),
        ],
        compiler_params=pltpu.CompilerParams(vmem_limit_bytes=VMEM_BYTES),
        name="corr",
    )(copies, scale, *halves)


def flip_rcv(x, bits):
    return lax.ppermute(x, "rcv", [(s, s ^ bits) for s in range(N_RCV)])


def own_half(x):
    place = lax.axis_index("rcv") % 4
    others = [flip_rcv(x, bits) for bits in (1, 2, 3)]
    half = jnp.zeros((x.shape[0], HALF), x.dtype)
    for bits, part in enumerate((x, *others)):
        half = lax.dynamic_update_slice(half, part, (0, (place ^ bits) * SEG))
    return half


def fetch(y, even, odd):
    pairs = [
        ((p + (odd if m % 2 else even)) % NB * N_RCV + m, p * N_RCV + m)
        for p in range(NB)
        for m in range(N_RCV)
    ]
    return lax.ppermute(y, ("src", "rcv"), pairs)


def second_fetch(own, a1, fourth):
    a2 = fetch(own, 7, fourth)
    return a2, flip_rcv(a1, 6), flip_rcv(a1, 1)


def on_device(traces, counts, distances):
    rows = jnp.concatenate(
        [traces, jnp.broadcast_to(counts.astype(jnp.bfloat16), (16, SEG))], axis=0
    )
    half = own_half(rows)
    own = half[:CB]
    a1 = fetch(own, -8, -1)
    fourth = jnp.sum(distances) - sum(FIXED)
    branch = jnp.where(fourth < 0, fourth + 7, fourth + 6)
    branch, ready = lax.optimization_barrier((branch, half))
    far_half = flip_rcv(ready, 6)
    moves = [functools.partial(second_fetch, fourth=d) for d in OTHERS]
    a2, c1, s1 = lax.switch(branch, moves, own, a1)
    c2 = flip_rcv(a2, 6)
    s2 = flip_rcv(a2, 1)
    r1 = flip_rcv(c1, 1)
    half, far_half, a2 = lax.optimization_barrier((half, far_half, a2))
    copies, scale = prepare(distances, half, far_half)
    c2, copies = lax.optimization_barrier((c2, copies))
    r2 = flip_rcv(c2, 1)
    halves = (a1, c1, a2, c2, s1, r1, s2, r2)
    return correlate(copies, scale, halves)[None]


def solution(mesh):
    in_specs = (P("src", "rcv"), P("src", "rcv"), P())
    out_specs = P("src", None, None, None, "rcv")
    return jax.shard_map(
        on_device, mesh=mesh, in_specs=in_specs, out_specs=out_specs, check_vma=False
    )
```

```python
import functools

import jax
import jax.numpy as jnp
from jax import lax
from jax.experimental import pallas as pl
from jax.experimental.pallas import tpu as pltpu
from jax.sharding import PartitionSpec as P

LAGS = 2048
VS = 64
WIN = 32
K = 4
CB = 128
SEG = 128
NB = 16
N_RCV = 8
TIME = 1024
SHARE = 256
HALF = 512
SPAN = TIME + SHARE
GROUP = 16
COPIES = 16
FIXED = (-8, -1, 7)
OTHERS = (-7, -6, -5, -4, -3, -2, 0, 1, 2, 3, 4, 5, 6)
VMEM_BYTES = 32 * 2**20


def whiten(raw):
    values = raw.astype(jnp.float32)
    energy = jnp.sum(values * values, axis=1, keepdims=True)
    return (values * lax.rsqrt(energy / TIME + 1e-06)).astype(jnp.bfloat16)


def at_end():
    part = lax.axis_index("rcv")
    return jnp.logical_or(part < 2, part >= N_RCV - 2)


def half_places(packed):
    half = lax.axis_index("rcv") // 4
    near = half * HALF
    if packed:
        near = jnp.where(at_end(), 0, near)
    return pl.multiple_of(near, HALF), pl.multiple_of(HALF - near, HALF)


def prepare_kernel(dist_ref, near_ref, far_ref, copies_ref, scale_ref, v_ref, own_ref):
    step = pl.program_id(0)

    @pl.when(step == 0)
    def _():
        near, far = half_places(False)
        own_ref[:, pl.ds(near, HALF)] = near_ref[...]
        own_ref[:, pl.ds(far, HALF)] = far_ref[...]
        counts = own_ref[CB : CB + 16, :].astype(jnp.float32)[0:1]
        norm = lax.rsqrt(jnp.sum(counts, axis=1, keepdims=True) * (WIN / SEG))
        line = lax.broadcasted_iota(jnp.int32, scale_ref.shape, 0)
        table = jnp.broadcast_to(norm, scale_ref.shape)
        for k in range(K):
            table = jnp.where(line == k + 1, dist_ref[k].astype(jnp.float32), table)
        scale_ref[...] = table
        lane = lax.broadcasted_iota(jnp.int32, (1, TIME), 1)
        kept = (lane % SEG).astype(jnp.float32) < counts * WIN
        sources = jnp.where(kept, whiten(own_ref[0:VS, :]).astype(jnp.float32), 0.0)
        sources = sources.astype(jnp.bfloat16)
        row = lax.broadcasted_iota(jnp.int32, (SEG, SEG), 0)
        col = lax.broadcasted_iota(jnp.int32, (SEG, SEG), 1)
        flip = jnp.where(row + col == SEG - 1, 1.0, 0.0).astype(jnp.bfloat16)
        v_ref[:, 0:TIME] = jnp.zeros((VS, TIME), jnp.float32)
        v_ref[:, 2 * TIME :] = jnp.zeros((VS, TIME), jnp.float32)
        for e in range(N_RCV):
            part = sources[:, (N_RCV - 1 - e) * SEG : (N_RCV - e) * SEG]
            v_ref[:, TIME + e * SEG : TIME + (e + 1) * SEG] = jnp.dot(
                part, flip, preferred_element_type=jnp.float32
            )

    part = lax.axis_index("rcv")
    late = jnp.where(part >= N_RCV - 2, HALF, 0)
    base = pl.multiple_of(part * SHARE - late, SHARE)
    first = pl.multiple_of(step * COPIES, COPIES)
    rows = v_ref[pl.ds(first, COPIES), pl.ds(base, SPAN)]
    spread = jnp.broadcast_to(rows[:, None, :], (COPIES, 16, SPAN))
    copies_ref[...] = pltpu.roll(spread, SPAN - 15, 2, stride=1, stride_axis=1).astype(jnp.bfloat16)


def prepare(distances, near, far):
    return pl.pallas_call(
        prepare_kernel,
        grid=(VS // COPIES,),
        in_specs=[
            pl.BlockSpec(memory_space=pltpu.SMEM),
            *[pl.BlockSpec((CB + 16, HALF), lambda i: (0, 0))] * 2,
        ],
        out_specs=[
            pl.BlockSpec((COPIES, 16, SPAN), lambda i: (i, 0, 0)),
            pl.BlockSpec((8, 128), lambda i: (0, 0)),
        ],
        out_shape=[
            jax.ShapeDtypeStruct((VS, 16, SPAN), jnp.bfloat16),
            jax.ShapeDtypeStruct((8, 128), jnp.float32),
        ],
        scratch_shapes=[
            pltpu.VMEM((VS, 3 * TIME), jnp.float32),
            pltpu.VMEM((CB + 16, TIME), jnp.bfloat16),
        ],
        compiler_params=pltpu.CompilerParams(vmem_limit_bytes=VMEM_BYTES),
        name="prepare",
    )(distances, near, far)


def corr_kernel(copies_ref, scale_ref, *refs):
    *halves, out_ref, w_ref, q_ref, plan_ref = refs

    @pl.when(pl.program_id(0) == 0)
    def _():
        core = lax.axis_index("rcv") % 2
        block = lax.axis_index("src")
        slot_of = [jnp.int32(0)] * K
        rest = jnp.int32(0)
        fourth = jnp.int32(0)
        for k in range(K):
            d = jnp.max(scale_ref[k + 1 : k + 2, :]).astype(jnp.int32)
            fixed = jnp.bool_(False)
            for s, known in enumerate(FIXED):
                hit = d == known
                slot_of[s] = jnp.where(hit, k, slot_of[s])
                fixed = jnp.logical_or(fixed, hit)
            rest = jnp.where(fixed, rest, k)
            fourth = jnp.where(fixed, fourth, d)
        slot_of[3] = rest
        order = ((0, 1), (2, 3), (1, 0), (3, 2))
        values = (*(jnp.int32(d) for d in FIXED), fourth)
        inside = []
        for x, y in order:
            partner = block + jnp.where(core == 0, values[x], values[y])
            inside.append(jnp.logical_and(partner >= 0, partner < NB).astype(jnp.int32))
        total = sum(inside)
        plan_ref[K] = total
        near, far = half_places(True)
        used, unused = jnp.int32(0), total
        for s, (x, y) in enumerate(order):
            rank = jnp.where(inside[s] == 1, used, unused)
            used, unused = used + inside[s], unused + 1 - inside[s]
            plan_ref[rank] = jnp.where(core == 0, slot_of[x], slot_of[y])
            first = halves[2 * s][...].astype(jnp.float32)
            second = halves[2 * s + 1][...].astype(jnp.float32)
            energy = jnp.sum(first * first + second * second, axis=1, keepdims=True)
            scale = lax.rsqrt(energy / TIME + 1e-06) * inside[s].astype(jnp.float32)
            rows = pl.ds(pl.multiple_of(rank * CB, CB), CB)
            w_ref[rows, pl.ds(near, HALF)] = (first * scale).astype(jnp.bfloat16)
            w_ref[rows, pl.ds(far, HALF)] = (second * scale).astype(jnp.bfloat16)

    scale = scale_ref[0:1, 0:1]
    slots = [plan_ref[r] for r in range(K)]
    total = plan_ref[K]
    end = at_end()

    def multiply(live, depth):
        count = depth // SEG + 1
        for ii in range(GROUP):
            copies = copies_ref[ii]
            blocks = q_ref.at[ii % 2]
            for g in range(8):
                for c in range(count):
                    at = 112 - 16 * g + SEG * (8 - c)
                    blocks[SEG * c + 16 * g : SEG * c + 16 * g + 16, :] = copies[:, at : at + SEG]
            tile = jnp.concatenate([blocks[SEG : SEG + depth], blocks[0:depth]], axis=1)
            summed = jnp.dot(
                w_ref[: live * CB, :depth], tile, preferred_element_type=jnp.float32
            )
            stack = (summed * scale).astype(jnp.bfloat16)
            for r in range(K):
                if r < live:
                    out_ref[slots[r], ii] = stack[r * CB : (r + 1) * CB]
                else:
                    out_ref[slots[r], ii] = jnp.zeros((CB, SHARE), jnp.bfloat16)

    for live in (2, 3, 4):
        fits = total <= 2 if live == 2 else total == live
        pl.when(jnp.logical_and(fits, end))(functools.partial(multiply, live, HALF))
        pl.when(jnp.logical_and(fits, jnp.logical_not(end)))(
            functools.partial(multiply, live, TIME)
        )


def correlate(copies, scale, halves):
    vmem = pl.BlockSpec((CB, HALF), lambda i: (0, 0))
    return pl.pallas_call(
        corr_kernel,
        grid=(VS // GROUP,),
        in_specs=[
            pl.BlockSpec((GROUP, 16, SPAN), lambda i: (i, 0, 0)),
            pl.BlockSpec((8, 128), lambda i: (0, 0)),
            *([vmem] * len(halves)),
        ],
        out_specs=pl.BlockSpec((K, GROUP, CB, SHARE), lambda i: (0, i, 0, 0)),
        out_shape=jax.ShapeDtypeStruct((K, VS, CB, SHARE), jnp.bfloat16),
        scratch_shapes=[
            pltpu.VMEM((K * CB, TIME), jnp.bfloat16),
            pltpu.VMEM((2, TIME + SEG, SEG), jnp.bfloat16),
            pltpu.SMEM((8,), jnp.int32),
        ],
        compiler_params=pltpu.CompilerParams(vmem_limit_bytes=VMEM_BYTES),
        name="corr",
    )(copies, scale, *halves)


def flip_rcv(x, bits):
    return lax.ppermute(x, "rcv", [(s, s ^ bits) for s in range(N_RCV)])


def own_half(x):
    place = lax.axis_index("rcv") % 4
    others = [flip_rcv(x, bits) for bits in (1, 2, 3)]
    half = jnp.zeros((x.shape[0], HALF), x.dtype)
    for bits, part in enumerate((x, *others)):
        half = lax.dynamic_update_slice(half, part, (0, (place ^ bits) * SEG))
    return half


def fetch(y, even, odd):
    pairs = [
        ((p + (odd if m % 2 else even)) % NB * N_RCV + m, p * N_RCV + m)
        for p in range(NB)
        for m in range(N_RCV)
    ]
    return lax.ppermute(y, ("src", "rcv"), pairs)


def second_fetch(own, a1, fourth):
    a2 = fetch(own, 7, fourth)
    return a2, flip_rcv(a1, 6), flip_rcv(a1, 1)


def on_device(traces, counts, distances):
    rows = jnp.concatenate(
        [traces, jnp.broadcast_to(counts.astype(jnp.bfloat16), (16, SEG))], axis=0
    )
    half = own_half(rows)
    own = half[:CB]
    a1 = fetch(own, -8, -1)
    fourth = jnp.sum(distances) - sum(FIXED)
    branch = jnp.where(fourth < 0, fourth + 7, fourth + 6)
    branch, ready = lax.optimization_barrier((branch, half))
    far_half = flip_rcv(ready, 6)
    moves = [functools.partial(second_fetch, fourth=d) for d in OTHERS]
    a2, c1, s1 = lax.switch(branch, moves, own, a1)
    c2 = flip_rcv(a2, 6)
    s2 = flip_rcv(a2, 1)
    r1 = flip_rcv(c1, 1)
    half, far_half, a2 = lax.optimization_barrier((half, far_half, a2))
    copies, scale = prepare(distances, half, far_half)
    c2, copies = lax.optimization_barrier((c2, copies))
    r2 = flip_rcv(c2, 1)
    halves = (a1, c1, a2, c2, s1, r1, s2, r2)
    return correlate(copies, scale, halves)[None]


def solution(mesh):
    in_specs = (P("src", "rcv"), P("src", "rcv"), P())
    out_specs = P("src", None, None, None, "rcv")
    return jax.shard_map(
        on_device, mesh=mesh, in_specs=in_specs, out_specs=out_specs, check_vma=False
    )
```
